1024 devices in a mesh: gy: 16 (over x, y_hi), gz: 64 (over z, y_lo, core).
Axes of the slice: x: 8, y: 8 (y_hi: 2, y_lo: 4; y = y_hi * 4 + y_lo), z: 8, core: 2. Of those that a mesh axis runs over, the one named last changes fastest.
Arguments:
- fields: float32 [8, 512, 128, 256], P(None, 'gz', 'gy'), may hold values from -5 to 5
- accum: float32 [8, 512, 128, 256], P(None, 'gz', 'gy'), may hold values from -4 to 4
Outputs:
- new_fields: float32 [8, 512, 128, 256], P(None, 'gz', 'gy')
- new_accum: float32 [8, 512, 128, 256], P(None, 'gz', 'gy')
- time_step: float32 [1], replicated
The draws below stay inside these ranges and needn't reach their ends.
All inputs are finite; a program needn't handle non-finite values.
Results may differ from the reference program's by a relative error of at most 0.0003.
Values sent between devices are 32-bit elements; how exact they have to be, the bound alone decides.
A program may use at most 32 MiB of HBM per device.

```python
import math
import jax
import jax.numpy as jnp
from jax import lax

NX = 256
CZ = 8
NFIELD = 8
NY = 128
NZ = 512


def draw_fields(key, part):
    key = jax.random.fold_in(key, 7)
    shape = (NFIELD, NZ, NY, NX)
    offset_z = jax.random.randint(jax.random.fold_in(key, 101), (), 0, NZ, dtype=jnp.int32)
    offset_y = jax.random.randint(jax.random.fold_in(key, 103), (), 0, NY, dtype=jnp.int32)
    place_z = (lax.broadcasted_iota(jnp.int32, shape, 1) + offset_z) % NZ
    place_y = (lax.broadcasted_iota(jnp.int32, shape, 2) + offset_y) % NY
    across_z = place_z.astype(jnp.float32) / NZ
    across_y = place_y.astype(jnp.float32) / NY
    kind = lax.broadcasted_iota(jnp.int32, shape, 0)
    base = jax.random.truncated_normal(key, -4.0, 4.0, shape, jnp.float32)
    lift = 0.0
    ramp = 0.1 * jnp.exp(math.log(3.0) * (across_z + across_y))
    moving = (kind >= 1) & (kind <= 3)
    scale = jnp.where(moving, ramp, jnp.where(kind >= 5, 0.3, 0.15))
    offset = jnp.where(kind == 4, lift, 0.0)
    return (base * scale + offset).astype(jnp.float32)


def shard_levels(stream_key, extent, cuts, least, largest):
    def one(axis_at, blocks):
        steps = jax.random.uniform(jax.random.fold_in(jax.random.fold_in(stream_key, 6), axis_at), (blocks,), jnp.float32, least / len(cuts), largest / len(cuts))
        return jnp.repeat(jnp.exp(steps), extent[axis_at] // blocks).reshape((-1,) + (1,) * (len(extent) - axis_at - 1))

    gain = one(*cuts[0])
    for cut in cuts[1:]:
        gain = gain * one(*cut)
    return gain


def gaussian(rng, extent, scale, most, cuts=(), held_as=jnp.bfloat16):
    loudness = shard_levels(rng, extent, cuts, -0.22, 0.18) if cuts else 1.0
    entries = jax.random.normal(rng, extent, jnp.float32) * scale * loudness
    return jnp.minimum(jnp.maximum(entries, -most), most).astype(held_as)


def setup_inputs(seed: int = 0) -> dict:
    key_of = jax.random.split(jax.random.key(seed), 3)
    fields = draw_fields(jax.random.fold_in(key_of[2], 71), 0)
    accum = gaussian(key_of[1], (NFIELD, NZ, NY, NX), 0.5, 4.0, ((1, 64), (2, 16)), jnp.float32)
    return dict(fields=fields, accum=accum)


def shifted(block, dim, step):
    count = block.shape[dim] - 6
    return lax.slice_in_dim(block, 3 + step, 3 + step + count, axis=dim)

def first_pad(block, dim):
    return (45.0 * (shifted(block, dim, 1) - shifted(block, dim, -1)) - 9.0 * (shifted(block, dim, 2) - shifted(block, dim, -2)) + (shifted(block, dim, 3) - shifted(block, dim, -3))) / 60.0

def second_pad(block, dim):
    return (-490.0 * shifted(block, dim, 0) + 270.0 * (shifted(block, dim, 1) + shifted(block, dim, -1)) - 27.0 * (shifted(block, dim, 2) + shifted(block, dim, -2)) + 2.0 * (shifted(block, dim, 3) + shifted(block, dim, -3))) / 180.0

def rolled(block, step):
    return jnp.roll(block, -step, axis=3)

def first_x(block):
    return (45.0 * (rolled(block, 1) - rolled(block, -1)) - 9.0 * (rolled(block, 2) - rolled(block, -2)) + (rolled(block, 3) - rolled(block, -3))) / 60.0

def second_x(block):
    return (-490.0 * block + 270.0 * (rolled(block, 1) + rolled(block, -1)) - 27.0 * (rolled(block, 2) + rolled(block, -2)) + 2.0 * (rolled(block, 3) + rolled(block, -3))) / 180.0

def tendency(padded):
    inner = padded[:, 3:-3, 3:-3]
    grad = (first_x(inner), first_pad(padded[:, 3:-3], 2), first_pad(padded[:, :, 3:-3], 1))
    diag = (second_x(inner), second_pad(padded[:, 3:-3], 2), second_pad(padded[:, :, 3:-3], 1))
    mixed_xy = first_x(grad[1])
    mixed_xz = first_x(grad[2])
    mixed_yz = first_pad(first_pad(padded, 1), 2)
    table = ((None, mixed_xy, mixed_xz), (mixed_xy, None, mixed_yz), (mixed_xz, mixed_yz, None))

    def hess(i, j, k):
        if i == j:
            return diag[i][k]
        return table[i][j][k]

    def lap(k):
        return diag[0][k] + diag[1][k] + diag[2][k]
    lnrho = inner[0]
    ss = inner[4]
    vel = [inner[1], inner[2], inner[3]]

    def dvel(i, j):
        return grad[j][1 + i]

    def dpot(i, j):
        return grad[j][5 + i]
    field_b = [dpot(2, 1) - dpot(1, 2), dpot(0, 2) - dpot(2, 0), dpot(1, 0) - dpot(0, 1)]
    current = [hess(i, 0, 5) + hess(i, 1, 6) + hess(i, 2, 7) - lap(5 + i) for i in range(3)]
    divu = dvel(0, 0) + dvel(1, 1) + dvel(2, 2)
    strain = [[0.5 * (dvel(i, j) + dvel(j, i)) - (divu / 3.0 if i == j else 0.0) for j in range(3)] for i in range(3)]
    reciprocal_mass_per_volume = jnp.exp(-lnrho)
    acoustic_wave_celerity = jnp.exp(5.0 / 3.0 * ss + 2.0 / 3.0 * lnrho)
    thermal_level = 1.5 * acoustic_wave_celerity

    def transport_flux(k):
        return vel[0] * grad[0][k] + vel[1] * grad[1][k] + vel[2] * grad[2][k]
    lorentz = [current[1] * field_b[2] - current[2] * field_b[1], current[2] * field_b[0] - current[0] * field_b[2], current[0] * field_b[1] - current[1] * field_b[0]]
    uxb = [vel[1] * field_b[2] - vel[2] * field_b[1], vel[2] * field_b[0] - vel[0] * field_b[2], vel[0] * field_b[1] - vel[1] * field_b[0]]
    total_change_rate = [-transport_flux(0) - divu]
    for i in range(3):
        viscous = lap(1 + i) + (hess(i, 0, 1) + hess(i, 1, 2) + hess(i, 2, 3)) / 3.0 + 2.0 * (strain[i][0] * grad[0][0] + strain[i][1] * grad[1][0] + strain[i][2] * grad[2][0])
        total_change_rate.append(-transport_flux(1 + i) - acoustic_wave_celerity * (grad[i][4] + grad[i][0]) + lorentz[i] * reciprocal_mass_per_volume + 0.1 * viscous)
    deformation_norm = sum((strain[i][j] * strain[i][j] for i in range(3) for j in range(3)))
    electric_flow_norm = current[0] * current[0] + current[1] * current[1] + current[2] * current[2]
    total_change_rate.append(-transport_flux(4) + (2.0 * 0.1 * deformation_norm + 0.1 * electric_flow_norm * reciprocal_mass_per_volume) / thermal_level)
    for i in range(3):
        total_change_rate.append(uxb[i] + 0.1 * lap(5 + i))
    b_sq = field_b[0] * field_b[0] + field_b[1] * field_b[1] + field_b[2] * field_b[2]
    rate = jnp.abs(vel[0]) + jnp.abs(vel[1]) + jnp.abs(vel[2]) + jnp.sqrt(acoustic_wave_celerity + b_sq * reciprocal_mass_per_volume)
    return (jnp.max(rate), jnp.stack(total_change_rate))

def reference(fields, accum):
    wrapped = jnp.concatenate([fields[:, -3:], fields, fields[:, :3]], axis=1)
    wrapped = jnp.concatenate([wrapped[:, :, -3:], wrapped, wrapped[:, :, :3]], axis=2)
    count = NZ // CZ

    def one(index):
        start = (index * CZ).astype(jnp.int32)
        piece = lax.dynamic_slice_in_dim(wrapped, start, CZ + 6, 1)
        return tendency(piece)
    rates, pieces = lax.map(one, jnp.arange(count, dtype=jnp.int32))
    rhs = jnp.moveaxis(pieces, 0, 1).reshape(fields.shape)
    time_step = 0.4 / jnp.max(rates)
    new_accum = -5.0 / 9.0 * accum + rhs
    new_fields = fields + 15.0 / 16.0 * time_step * new_accum
    return (new_fields, new_accum, jnp.reshape(time_step, (1,)))
```

```python
import jax
import jax.numpy as jnp
from jax import lax
from jax.experimental import pallas as pl
from jax.experimental.pallas import tpu as pltpu
from jax.sharding import PartitionSpec as P

MESH = pl.DeviceIdType.MESH
F32 = jnp.float32
MIXED = (2, 3, 6, 7)
X_SHIFT = 2
FAN = 32


def place():
    gy = lax.axis_index("gy")
    gz = lax.axis_index("gz")
    xs = lax.rem(gy // 2 + X_SHIFT, 8)
    y = lax.rem(gy, 2) * 4 + lax.rem(gz // 2, 4)
    return xs, y, gz // 8, lax.rem(gz, 2)


def device(xs, y, z, core):
    x = lax.rem(xs + 8 - X_SHIFT, 8)
    return (x * 2 + y // 4, (z * 4 + lax.rem(y, 4)) * 2 + core)


def member(leader, index):
    xs, y, core = leader
    return device(lax.rem(xs, 4) + 4 * (index // 16), lax.rem(y, 4) + 4 * lax.rem(index // 8, 2), lax.rem(index, 8), core)


ROOT = 17


def chief(index):
    at = lax.rem(index + ROOT, FAN)
    return device(at // 8, lax.rem(at // 2, 4), 0, lax.rem(at, 2))


def x_shift(t, s):
    return pltpu.roll(t, (256 - s) % 256, 1)


def y_shift(t, h, s):
    row = lax.broadcasted_iota(jnp.int32, t.shape, 0)
    if s > 0:
        return pltpu.roll(jnp.where(row < s, h, t), 8 - s, 0)
    return pltpu.roll(jnp.where(row >= 8 + s, h, t), -s, 0)


def first_of(f):
    return (
        (45.0 / 60.0) * (f(1) - f(-1))
        - (9.0 / 60.0) * (f(2) - f(-2))
        + (1.0 / 60.0) * (f(3) - f(-3))
    )


def second_of(f):
    return (
        (-490.0 / 180.0) * f(0)
        + (270.0 / 180.0) * (f(1) + f(-1))
        - (27.0 / 180.0) * (f(2) + f(-2))
        + (2.0 / 180.0) * (f(3) + f(-3))
    )


def memo(f):
    held = {}

    def get(s):
        if s not in held:
            held[s] = f(s)
        return held[s]

    return get


def along_x(t):
    return memo(lambda s: t if s == 0 else x_shift(t, s))


def substep(
    f_hbm,
    a_hbm,
    na_ref,
    top_ref,
    F,
    A,
    H,
    GY,
    B,
    J,
    own,
    ups,
    chiefs,
    down,
    load_sem,
    y_send,
    y_recv,
    z_send,
    z_recv,
    g_send,
    g_recv,
    t_send,
    t_recv,
):
    gy = lax.axis_index("gy")
    gz = lax.axis_index("gz")
    up_y, down_y = lax.rem(gy + 1, 16), lax.rem(gy + 15, 16)
    up_z, down_z = lax.rem(gz + 1, 64), lax.rem(gz + 63, 64)
    xs, y, z, core = place()
    in_group = (xs // 4) * 16 + (y // 4) * 8 + z
    among_chiefs = lax.rem(lax.rem(xs, 4) * 8 + lax.rem(y, 4) * 2 + core + FAN - ROOT, FAN)
    is_chief = in_group == 0
    is_root = jnp.logical_and(is_chief, among_chiefs == 0)
    group = (xs, y, core)

    load_f = pltpu.make_async_copy(f_hbm, F.at[:, pl.ds(3, 8)], load_sem.at[0])
    load_a = pltpu.make_async_copy(a_hbm, A, load_sem.at[1])
    load_f.start()
    load_a.start()

    barrier = pltpu.get_barrier_semaphore()
    for to in ((up_y, gz), (down_y, gz), (gy, up_z), (gy, down_z)):
        pl.semaphore_signal(barrier, inc=1, device_id=to, device_id_type=MESH)

    @pl.when(is_root)
    def _():
        def tell(i, c):
            pl.semaphore_signal(barrier, inc=1, device_id=chief(i), device_id_type=MESH)
            return c

        lax.fori_loop(0, FAN, tell, 0)

    @pl.when(is_chief)
    def _():
        def tell(i, c):
            pl.semaphore_signal(barrier, inc=1, device_id=member(group, i), device_id_type=MESH)
            return c

        lax.fori_loop(1, FAN, tell, 0)

    pl.semaphore_wait(barrier, 5)

    def remote(src, dst, send, recv, to):
        return pltpu.make_async_remote_copy(
            src_ref=src, dst_ref=dst, send_sem=send, recv_sem=recv, device_id=to, device_id_type=MESH
        )

    halos = []
    for part, (start, count) in enumerate(((5, 3), (0, 5))):
        ks = pl.ds(start, count)
        low, high = pl.ds(0, 3), pl.ds(5, 3)
        halos.append(
            [
                remote(f_hbm.at[ks, :, low], H.at[ks, :, low], y_send.at[0, part], y_recv.at[0, part], (down_y, gz)),
                remote(f_hbm.at[ks, :, high], H.at[ks, :, high], y_send.at[1, part], y_recv.at[1, part], (up_y, gz)),
                remote(f_hbm.at[ks, low], F.at[ks, pl.ds(11, 3)], z_send.at[0, part], z_recv.at[0, part], (gy, down_z)),
                remote(f_hbm.at[ks, high], F.at[ks, pl.ds(0, 3)], z_send.at[1, part], z_recv.at[1, part], (gy, up_z)),
            ]
        )
    for part in halos:
        for copy in part:
            copy.start()

    def along_y(k, i):
        t, h = F[k, i + 3], H[k, i]
        return memo(lambda s: t if s == 0 else y_shift(t, h, s))

    def along_z(k, i):
        return lambda s: F[k, i + 3 + s]

    load_f.wait()
    for copy in halos[0]:
        copy.wait_recv()

    own[...] = jnp.zeros_like(own)

    def rates(i, c):
        t = [F[k, i + 3] for k in range(8)]
        bx = first_of(along_y(7, i)) - first_of(along_z(6, i))
        by = first_of(along_z(5, i)) - first_of(along_x(t[7]))
        bz = first_of(along_x(t[6])) - first_of(along_y(5, i))
        B[0, i] = bx
        B[1, i] = by
        B[2, i] = bz
        cs2 = jnp.exp((5.0 / 3.0) * t[4] + (2.0 / 3.0) * t[0])
        inverse = jnp.exp(-t[0])
        rate = (
            jnp.abs(t[1])
            + jnp.abs(t[2])
            + jnp.abs(t[3])
            + jnp.sqrt(cs2 + (bx * bx + by * by + bz * bz) * inverse)
        )
        own[...] = jnp.maximum(own[...], jnp.maximum(rate[:, :128], rate[:, 128:]))
        return c

    lax.fori_loop(0, 8, rates, 0)

    to_chief = remote(own, ups.at[in_group], t_send.at[0], t_recv.at[0], member(group, 0))

    @pl.when(jnp.logical_not(is_chief))
    def _():
        to_chief.start()

    for copy in halos[1]:
        copy.wait_recv()

    def slopes(i, c):
        for j, k in enumerate(MIXED):
            GY[j, i + 3] = first_of(along_y(k, i))
        return c

    lax.fori_loop(0, 8, slopes, 0)
    edges = [
        remote(GY.at[:, pl.ds(3, 3)], GY.at[:, pl.ds(11, 3)], g_send.at[0], g_recv.at[0], (gy, down_z)),
        remote(GY.at[:, pl.ds(8, 3)], GY.at[:, pl.ds(0, 3)], g_send.at[1], g_recv.at[1], (gy, up_z)),
    ]
    for copy in edges:
        copy.start()
    load_a.wait()

    def partial(i, c):
        t = [F[k, i + 3] for k in range(8)]
        ax = [along_x(t[k]) for k in range(8)]
        ay = [along_y(k, i) for k in range(8)]
        az = [along_z(k, i) for k in range(8)]
        dx = {k: first_of(ax[k]) for k in range(5)}
        dy = {k: GY[MIXED.index(k), i + 3] if k in MIXED else first_of(ay[k]) for k in range(7)}
        dz = {k: first_of(az[k]) for k in (0, 1, 2, 3, 4, 5, 7)}
        u = t[1:4]
        bx, by, bz = B[0, i], B[1, i], B[2, i]

        def put(k, value):
            na_ref[k, i] = (-5.0 / 9.0) * A[k, i] + value

        def advect(k):
            return u[0] * dx[k] + u[1] * dy[k] + u[2] * dz[k]

        divu = dx[1] + dy[2] + dz[3]
        third = divu * (1.0 / 3.0)
        sxx, syy, szz = dx[1] - third, dy[2] - third, dz[3] - third
        sxy = 0.5 * (dy[1] + dx[2])
        sxz = 0.5 * (dz[1] + dx[3])
        syz = 0.5 * (dz[2] + dy[3])
        cs2 = jnp.exp((5.0 / 3.0) * t[4] + (2.0 / 3.0) * t[0])
        put(0, -advect(0) - divu)
        strain = ((sxx, sxy, sxz), (sxy, syy, syz), (sxz, syz, szz))
        xx = second_of(ax[1]), second_of(ax[2]), second_of(ax[3])
        yy = second_of(ay[1]), second_of(ay[2]), second_of(ay[3])
        zz = second_of(az[1]), second_of(az[2]), second_of(az[3])
        mixed = (
            xx[0] + first_of(along_x(dy[2])) + first_of(along_x(dz[3])),
            yy[1] + first_of(along_x(dy[1])),
            zz[2] + first_of(along_x(dz[1])),
        )
        grad = (dx, dy, dz)
        for n in range(3):
            viscous = (
                xx[n]
                + yy[n]
                + zz[n]
                + mixed[n] * (1.0 / 3.0)
                + 2.0 * (strain[n][0] * dx[0] + strain[n][1] * dy[0] + strain[n][2] * dz[0])
            )
            put(1 + n, -advect(1 + n) - cs2 * (grad[n][4] + grad[n][0]) + 0.1 * viscous)
        norm = sxx * sxx + syy * syy + szz * szz + 2.0 * (sxy * sxy + sxz * sxz + syz * syz)
        put(4, -advect(4) + 0.2 * norm / (1.5 * cs2))

        xx = second_of(ax[5]), second_of(ax[6]), second_of(ax[7])
        yy = second_of(ay[5]), second_of(ay[6]), second_of(ay[7])
        zz = second_of(az[5]), second_of(az[6]), second_of(az[7])
        J[0, i] = first_of(along_x(dy[6])) + first_of(along_x(dz[7])) - yy[0] - zz[0]
        J[1, i] = first_of(along_x(dy[5])) - xx[1] - zz[1]
        J[2, i] = first_of(along_x(dz[5])) - xx[2] - yy[2]
        cross = (u[1] * bz - u[2] * by, u[2] * bx - u[0] * bz, u[0] * by - u[1] * bx)
        for n in range(3):
            put(5 + n, cross[n] + 0.1 * (xx[n] + yy[n] + zz[n]))
        return c

    lax.fori_loop(0, 8, partial, 0)

    for copy in edges:
        copy.wait_recv()

    def finish(i, c):
        yz = [first_of(lambda s, j=j: GY[j, i + 3 + s]) for j in range(4)]
        bx, by, bz = B[0, i], B[1, i], B[2, i]
        jx, jy, jz = J[0, i], J[1, i] + yz[3], J[2, i] + yz[2]
        inverse = jnp.exp(-F[0, i + 3])
        cs2 = jnp.exp((5.0 / 3.0) * F[4, i + 3] + (2.0 / 3.0) * F[0, i + 3])
        na_ref[1, i] = na_ref[1, i] + (jy * bz - jz * by) * inverse
        na_ref[2, i] = na_ref[2, i] + (jz * bx - jx * bz) * inverse + (0.1 / 3.0) * yz[1]
        na_ref[3, i] = na_ref[3, i] + (jx * by - jy * bx) * inverse + (0.1 / 3.0) * yz[0]
        na_ref[4, i] = na_ref[4, i] + 0.1 * (jx * jx + jy * jy + jz * jz) * inverse / (1.5 * cs2)
        return c

    lax.fori_loop(0, 8, finish, 0)

    to_root = remote(own, chiefs.at[among_chiefs], t_send.at[1], t_recv.at[1], chief(0))
    all_ups = remote(ups.at[pl.ds(1, FAN - 1)], ups.at[pl.ds(1, FAN - 1)], t_send.at[2], t_recv.at[0], chief(0))
    all_chiefs = remote(chiefs.at[pl.ds(1, FAN - 1)], chiefs.at[pl.ds(1, FAN - 1)], t_send.at[3], t_recv.at[1], chief(0))
    to_down = remote(down, down, t_send.at[2], t_recv.at[2], chief(0))

    @pl.when(is_chief)
    def _():
        all_ups.wait_recv()
        own[...] = jnp.maximum(own[...], jnp.max(ups[1:], axis=0))

        @pl.when(jnp.logical_not(is_root))
        def _():
            to_root.start()

    @pl.when(is_root)
    def _():
        all_chiefs.wait_recv()
        most = jnp.max(jnp.maximum(own[...], jnp.max(chiefs[1:], axis=0)))
        down[...] = jnp.full(down.shape, most, F32)

        def tell(i, c):
            remote(down, down, t_send.at[3], t_recv.at[2], chief(i)).start()
            return c

        lax.fori_loop(1, FAN, tell, 0)

    @pl.when(jnp.logical_not(is_root))
    def _():
        to_down.wait_recv()

    @pl.when(is_chief)
    def _():
        def tell(i, c):
            remote(down, down, t_send.at[2], t_recv.at[2], member(group, i)).start()
            return c

        lax.fori_loop(1, FAN, tell, 0)

    top_ref[...] = down[...]

    for part in halos:
        for copy in part:
            copy.wait_send()
    for copy in edges:
        copy.wait_send()

    @pl.when(jnp.logical_not(is_chief))
    def _():
        to_chief.wait_send()

    @pl.when(is_chief)
    def _():
        all_ups.wait_send()

        @pl.when(jnp.logical_not(is_root))
        def _():
            to_root.wait_send()

    @pl.when(is_root)
    def _():
        all_chiefs.wait_send()


def update(f_ref, na_ref, top_ref, nf_ref, out_ref, dt_ref):
    dt = 0.4 / top_ref[...]
    dt_ref[0] = dt[0, 0]
    scale = (15.0 / 16.0) * dt[0:1, 0:1]
    na = na_ref[...]
    out_ref[...] = na
    nf_ref[...] = f_ref[...] + scale[None, None] * na


def local(fields, accum):
    block = jax.ShapeDtypeStruct(fields.shape, F32)
    vmem = pl.BlockSpec(memory_space=pltpu.VMEM)
    anywhere = pl.BlockSpec(memory_space=pl.ANY)
    na, top = pl.pallas_call(
        substep,
        out_shape=(block, jax.ShapeDtypeStruct((8, 128), F32)),
        in_specs=[anywhere, anywhere],
        out_specs=(vmem, vmem),
        scratch_shapes=[
            pltpu.VMEM((8, 14, 8, 256), F32),
            pltpu.VMEM((8, 8, 8, 256), F32),
            pltpu.VMEM((8, 8, 8, 256), F32),
            pltpu.VMEM((4, 14, 8, 256), F32),
            pltpu.VMEM((3, 8, 8, 256), F32),
            pltpu.VMEM((3, 8, 8, 256), F32),
            pltpu.VMEM((8, 128), F32),
            pltpu.VMEM((FAN, 8, 128), F32),
            pltpu.VMEM((FAN, 8, 128), F32),
            pltpu.VMEM((8, 128), F32),
            pltpu.SemaphoreType.DMA((2,)),
            pltpu.SemaphoreType.DMA((2, 2)),
            pltpu.SemaphoreType.DMA((2, 2)),
            pltpu.SemaphoreType.DMA((2, 2)),
            pltpu.SemaphoreType.DMA((2, 2)),
            pltpu.SemaphoreType.DMA((2,)),
            pltpu.SemaphoreType.DMA((2,)),
            pltpu.SemaphoreType.DMA((4,)),
            pltpu.SemaphoreType.DMA((3,)),
        ],
        compiler_params=pltpu.CompilerParams(
            collective_id=0, has_side_effects=True, vmem_limit_bytes=60 * 1024 * 1024
        ),
        cost_estimate=pl.CostEstimate(flops=13_000_000, bytes_accessed=2_000_000, transcendentals=100_000),
    )(fields, accum)
    return pl.pallas_call(
        update,
        out_shape=(block, block, jax.ShapeDtypeStruct((1,), F32)),
        in_specs=[vmem, vmem, vmem],
        out_specs=(vmem, vmem, pl.BlockSpec(memory_space=pltpu.SMEM)),
        compiler_params=pltpu.CompilerParams(vmem_limit_bytes=32 * 1024 * 1024),
        cost_estimate=pl.CostEstimate(flops=300_000, bytes_accessed=2_500_000, transcendentals=0),
    )(fields, na, top)


def solution(mesh):
    in_specs = (P(None, "gz", "gy", None), P(None, "gz", "gy", None))
    out_specs = (P(None, "gz", "gy", None), P(None, "gz", "gy", None), P())
    return jax.shard_map(local, mesh=mesh, in_specs=in_specs, out_specs=out_specs, check_vma=False)
```

```python
import jax
import jax.numpy as jnp
from jax import lax
from jax.experimental import pallas as pl
from jax.experimental.pallas import tpu as pltpu
from jax.sharding import PartitionSpec as P

MESH = pl.DeviceIdType.MESH
F32 = jnp.float32
MIXED = (2, 3, 6, 7)
COLUMN = 8
PLANE = 128


def chief(index):
    at = (index + 1) % PLANE
    return at // 8, at % 8


def hops(index):
    gy, gz = chief(index)
    x, y = gy // 2, gy % 2 * 4 + gz // 2
    return min(x, 8 - x) + min(y, 8 - y)


NEAR_FIRST = sorted(range(1, PLANE), key=hops)


def x_shift(t, s):
    return pltpu.roll(t, (256 - s) % 256, 1)


def y_shift(t, h, s):
    row = lax.broadcasted_iota(jnp.int32, t.shape, 0)
    if s > 0:
        return pltpu.roll(jnp.where(row < s, h, t), 8 - s, 0)
    return pltpu.roll(jnp.where(row >= 8 + s, h, t), -s, 0)


def first_of(f):
    return (
        (45.0 / 60.0) * (f(1) - f(-1))
        - (9.0 / 60.0) * (f(2) - f(-2))
        + (1.0 / 60.0) * (f(3) - f(-3))
    )


def second_of(f):
    return (
        (-490.0 / 180.0) * f(0)
        + (270.0 / 180.0) * (f(1) + f(-1))
        - (27.0 / 180.0) * (f(2) + f(-2))
        + (2.0 / 180.0) * (f(3) + f(-3))
    )


def memo(f):
    held = {}

    def get(s):
        if s not in held:
            held[s] = f(s)
        return held[s]

    return get


def along_x(t):
    return memo(lambda s: t if s == 0 else x_shift(t, s))


def substep(
    f_hbm,
    a_hbm,
    na_ref,
    top_ref,
    F,
    A,
    H,
    GY,
    B,
    J,
    tile,
    own,
    ups,
    chiefs,
    down,
    load_sem,
    y_send,
    y_recv,
    z_send,
    z_recv,
    g_send,
    g_recv,
    t_send,
    t_recv,
):
    gy = lax.axis_index("gy")
    gz = lax.axis_index("gz")
    up_y, down_y = lax.rem(gy + 1, 16), lax.rem(gy + 15, 16)
    up_z, down_z = lax.rem(gz + 1, 64), lax.rem(gz + 63, 64)
    level = gz // 8
    among = lax.rem(gy * 8 + gz + PLANE - 1, PLANE)
    is_chief = level == 0
    is_root = jnp.logical_and(gy == 0, gz == 1)

    load_f = pltpu.make_async_copy(f_hbm, F.at[:, pl.ds(3, 8)], load_sem.at[0])
    load_a = pltpu.make_async_copy(a_hbm, A, load_sem.at[1])
    load_f.start()
    load_a.start()

    barrier = pltpu.get_barrier_semaphore()
    for to in ((up_y, gz), (down_y, gz), (gy, up_z), (gy, down_z)):
        pl.semaphore_signal(barrier, inc=1, device_id=to, device_id_type=MESH)

    @pl.when(is_root)
    def _():
        for i in [0, *NEAR_FIRST]:
            pl.semaphore_signal(barrier, inc=1, device_id=chief(i), device_id_type=MESH)

    @pl.when(is_chief)
    def _():
        for i in range(1, COLUMN):
            pl.semaphore_signal(barrier, inc=1, device_id=(gy, gz + 8 * i), device_id_type=MESH)

    pl.semaphore_wait(barrier, 5)

    def remote(src, dst, send, recv, to):
        return pltpu.make_async_remote_copy(
            src_ref=src, dst_ref=dst, send_sem=send, recv_sem=recv, device_id=to, device_id_type=MESH
        )

    low, high = pl.ds(0, 3), pl.ds(5, 3)

    def y_halo(part, start, count):
        ks = pl.ds(start, count)
        return [
            remote(f_hbm.at[ks, :, low], H.at[ks, :, low], y_send.at[0, part], y_recv.at[0, part], (down_y, gz)),
            remote(f_hbm.at[ks, :, high], H.at[ks, :, high], y_send.at[1, part], y_recv.at[1, part], (up_y, gz)),
        ]

    def z_halo(part, start, count):
        ks = pl.ds(start, count)
        return [
            remote(f_hbm.at[ks, low], F.at[ks, pl.ds(11, 3)], z_send.at[0, part], z_recv.at[0, part], (gy, down_z)),
            remote(f_hbm.at[ks, high], F.at[ks, pl.ds(0, 3)], z_send.at[1, part], z_recv.at[1, part], (gy, up_z)),
        ]

    first = y_halo(0, 5, 1) + y_halo(1, 7, 1) + z_halo(0, 5, 2)
    then_y = y_halo(2, 6, 1) + y_halo(3, 2, 2)
    then_z = z_halo(1, 7, 1) + z_halo(2, 0, 5)
    last_y = y_halo(4, 0, 2) + y_halo(5, 4, 1)
    for copy in first + then_z:
        copy.start()
    for copy in first:
        copy.wait_send()
    for copy in then_y:
        copy.start()

    def along_y(k, i):
        t, h = F[k, i + 3], H[k, i]
        return memo(lambda s: t if s == 0 else y_shift(t, h, s))

    def along_z(k, i):
        return lambda s: F[k, i + 3 + s]

    load_f.wait()
    for copy in first:
        copy.wait_recv()

    tile[...] = jnp.zeros_like(tile)

    def rates(i, c):
        t = [F[k, i + 3] for k in range(8)]
        bx = first_of(along_y(7, i)) - first_of(along_z(6, i))
        by = first_of(along_z(5, i)) - first_of(along_x(t[7]))
        bz = first_of(along_x(t[6])) - first_of(along_y(5, i))
        B[0, i] = bx
        B[1, i] = by
        B[2, i] = bz
        cs2 = jnp.exp((5.0 / 3.0) * t[4] + (2.0 / 3.0) * t[0])
        inverse = jnp.exp(-t[0])
        rate = (
            jnp.abs(t[1])
            + jnp.abs(t[2])
            + jnp.abs(t[3])
            + jnp.sqrt(cs2 + (bx * bx + by * by + bz * bz) * inverse)
        )
        tile[...] = jnp.maximum(tile[...], jnp.maximum(rate[:, :128], rate[:, 128:]))
        return c

    lax.fori_loop(0, 8, rates, 0)

    own[...] = jnp.max(tile[...], axis=0, keepdims=True)
    chief_id = (gy, lax.rem(gz, 8))
    to_chief = remote(own, ups.at[level], t_send.at[0], t_recv.at[0], chief_id)
    all_ups = remote(ups.at[pl.ds(1, COLUMN - 1)], ups.at[pl.ds(1, COLUMN - 1)], t_send.at[2], t_recv.at[0], chief_id)
    to_root = remote(own, chiefs.at[among], t_send.at[1], t_recv.at[1], chief(0))
    all_chiefs = remote(chiefs.at[pl.ds(1, PLANE - 1)], chiefs.at[pl.ds(1, PLANE - 1)], t_send.at[3], t_recv.at[1], chief(0))
    to_down = remote(down, down, t_send.at[2], t_recv.at[2], chief(0))

    @pl.when(jnp.logical_not(is_chief))
    def _():
        to_chief.start()

    @pl.when(is_chief)
    def _():
        all_ups.wait_recv()
        own[...] = jnp.maximum(own[...], jnp.max(ups[1:], axis=0))

        @pl.when(jnp.logical_not(is_root))
        def _():
            to_root.start()

    for copy in then_y:
        copy.wait_recv()

    def slopes(i, c):
        for j, k in enumerate(MIXED):
            GY[j, i + 3] = first_of(along_y(k, i))
        return c

    lax.fori_loop(0, 8, slopes, 0)
    edges = [
        remote(GY.at[:, pl.ds(3, 3)], GY.at[:, pl.ds(11, 3)], g_send.at[0], g_recv.at[0], (gy, down_z)),
        remote(GY.at[:, pl.ds(8, 3)], GY.at[:, pl.ds(0, 3)], g_send.at[1], g_recv.at[1], (gy, up_z)),
    ]
    for copy in edges + last_y:
        copy.start()
    load_a.wait()
    for copy in then_z + last_y:
        copy.wait_recv()

    def partial(i, c):
        t = [F[k, i + 3] for k in range(8)]
        ax = [along_x(t[k]) for k in range(8)]
        ay = [along_y(k, i) for k in range(8)]
        az = [along_z(k, i) for k in range(8)]
        dx = {k: first_of(ax[k]) for k in range(5)}
        dy = {k: GY[MIXED.index(k), i + 3] if k in MIXED else first_of(ay[k]) for k in range(7)}
        dz = {k: first_of(az[k]) for k in (0, 1, 2, 3, 4, 5, 7)}
        u = t[1:4]
        bx, by, bz = B[0, i], B[1, i], B[2, i]

        def put(k, value):
            na_ref[k, i] = (-5.0 / 9.0) * A[k, i] + value

        def advect(k):
            return u[0] * dx[k] + u[1] * dy[k] + u[2] * dz[k]

        divu = dx[1] + dy[2] + dz[3]
        third = divu * (1.0 / 3.0)
        sxx, syy, szz = dx[1] - third, dy[2] - third, dz[3] - third
        sxy = 0.5 * (dy[1] + dx[2])
        sxz = 0.5 * (dz[1] + dx[3])
        syz = 0.5 * (dz[2] + dy[3])
        cs2 = jnp.exp((5.0 / 3.0) * t[4] + (2.0 / 3.0) * t[0])
        put(0, -advect(0) - divu)
        strain = ((sxx, sxy, sxz), (sxy, syy, syz), (sxz, syz, szz))
        xx = second_of(ax[1]), second_of(ax[2]), second_of(ax[3])
        yy = second_of(ay[1]), second_of(ay[2]), second_of(ay[3])
        zz = second_of(az[1]), second_of(az[2]), second_of(az[3])
        mixed = (
            xx[0] + first_of(along_x(dy[2])) + first_of(along_x(dz[3])),
            yy[1] + first_of(along_x(dy[1])),
            zz[2] + first_of(along_x(dz[1])),
        )
        grad = (dx, dy, dz)
        for n in range(3):
            viscous = (
                xx[n]
                + yy[n]
                + zz[n]
                + mixed[n] * (1.0 / 3.0)
                + 2.0 * (strain[n][0] * dx[0] + strain[n][1] * dy[0] + strain[n][2] * dz[0])
            )
            put(1 + n, -advect(1 + n) - cs2 * (grad[n][4] + grad[n][0]) + 0.1 * viscous)
        norm = sxx * sxx + syy * syy + szz * szz + 2.0 * (sxy * sxy + sxz * sxz + syz * syz)
        put(4, -advect(4) + 0.2 * norm / (1.5 * cs2))

        xx = second_of(ax[5]), second_of(ax[6]), second_of(ax[7])
        yy = second_of(ay[5]), second_of(ay[6]), second_of(ay[7])
        zz = second_of(az[5]), second_of(az[6]), second_of(az[7])
        J[0, i] = first_of(along_x(dy[6])) + first_of(along_x(dz[7])) - yy[0] - zz[0]
        J[1, i] = first_of(along_x(dy[5])) - xx[1] - zz[1]
        J[2, i] = first_of(along_x(dz[5])) - xx[2] - yy[2]
        cross = (u[1] * bz - u[2] * by, u[2] * bx - u[0] * bz, u[0] * by - u[1] * bx)
        for n in range(3):
            put(5 + n, cross[n] + 0.1 * (xx[n] + yy[n] + zz[n]))
        return c

    lax.fori_loop(0, 8, partial, 0)

    for copy in edges:
        copy.wait_recv()

    def finish(i, c):
        yz = [first_of(lambda s, j=j: GY[j, i + 3 + s]) for j in range(4)]
        bx, by, bz = B[0, i], B[1, i], B[2, i]
        jx, jy, jz = J[0, i], J[1, i] + yz[3], J[2, i] + yz[2]
        inverse = jnp.exp(-F[0, i + 3])
        cs2 = jnp.exp((5.0 / 3.0) * F[4, i + 3] + (2.0 / 3.0) * F[0, i + 3])
        na_ref[1, i] = na_ref[1, i] + (jy * bz - jz * by) * inverse
        na_ref[2, i] = na_ref[2, i] + (jz * bx - jx * bz) * inverse + (0.1 / 3.0) * yz[1]
        na_ref[3, i] = na_ref[3, i] + (jx * by - jy * bx) * inverse + (0.1 / 3.0) * yz[0]
        na_ref[4, i] = na_ref[4, i] + 0.1 * (jx * jx + jy * jy + jz * jz) * inverse / (1.5 * cs2)
        return c

    lax.fori_loop(0, 8, finish, 0)

    @pl.when(is_root)
    def _():
        all_chiefs.wait_recv()
        most = jnp.max(jnp.maximum(own[...], jnp.max(chiefs[1:], axis=0)))
        down[...] = jnp.full(down.shape, most, F32)
        for i in NEAR_FIRST:
            remote(down, down, t_send.at[3], t_recv.at[2], chief(i)).start()

    @pl.when(jnp.logical_not(is_root))
    def _():
        to_down.wait_recv()

    @pl.when(is_chief)
    def _():
        for i in range(1, COLUMN):
            remote(down, down, t_send.at[2], t_recv.at[2], (gy, gz + 8 * i)).start()

    top_ref[...] = down[...]

    for copy in then_y + then_z + last_y + edges:
        copy.wait_send()

    @pl.when(jnp.logical_not(is_chief))
    def _():
        to_chief.wait_send()

    @pl.when(is_chief)
    def _():
        all_ups.wait_send()

        @pl.when(jnp.logical_not(is_root))
        def _():
            to_root.wait_send()

    @pl.when(is_root)
    def _():
        all_chiefs.wait_send()


def update(f_ref, na_ref, top_ref, nf_ref, out_ref, dt_ref):
    dt = 0.4 / top_ref[...]
    dt_ref[0] = dt[0, 0]
    scale = (15.0 / 16.0) * dt[:, 0:1]
    na = na_ref[...]
    out_ref[...] = na
    nf_ref[...] = f_ref[...] + scale[None, None] * na


def local(fields, accum):
    block = jax.ShapeDtypeStruct(fields.shape, F32)
    vmem = pl.BlockSpec(memory_space=pltpu.VMEM)
    anywhere = pl.BlockSpec(memory_space=pl.ANY)
    na, top = pl.pallas_call(
        substep,
        out_shape=(pltpu.VMEM(fields.shape, F32), pltpu.VMEM((1, 128), F32)),
        in_specs=[anywhere, anywhere],
        out_specs=(vmem, vmem),
        scratch_shapes=[
            pltpu.VMEM((8, 14, 8, 256), F32),
            pltpu.VMEM((8, 8, 8, 256), F32),
            pltpu.VMEM((8, 8, 8, 256), F32),
            pltpu.VMEM((4, 14, 8, 256), F32),
            pltpu.VMEM((3, 8, 8, 256), F32),
            pltpu.VMEM((3, 8, 8, 256), F32),
            pltpu.VMEM((8, 128), F32),
            pltpu.VMEM((1, 128), F32),
            pltpu.VMEM((COLUMN, 1, 128), F32),
            pltpu.VMEM((PLANE, 1, 128), F32),
            pltpu.VMEM((1, 128), F32),
            pltpu.SemaphoreType.DMA((2,)),
            pltpu.SemaphoreType.DMA((2, 6)),
            pltpu.SemaphoreType.DMA((2, 6)),
            pltpu.SemaphoreType.DMA((2, 3)),
            pltpu.SemaphoreType.DMA((2, 3)),
            pltpu.SemaphoreType.DMA((2,)),
            pltpu.SemaphoreType.DMA((2,)),
            pltpu.SemaphoreType.DMA((4,)),
            pltpu.SemaphoreType.DMA((3,)),
        ],
        compiler_params=pltpu.CompilerParams(
            collective_id=0, has_side_effects=True, vmem_limit_bytes=60 * 1024 * 1024
        ),
        cost_estimate=pl.CostEstimate(flops=13_000_000, bytes_accessed=2_000_000, transcendentals=100_000),
    )(fields, accum)
    return pl.pallas_call(
        update,
        out_shape=(block, block, jax.ShapeDtypeStruct((1,), F32)),
        in_specs=[vmem, vmem, vmem],
        out_specs=(vmem, vmem, pl.BlockSpec(memory_space=pltpu.SMEM)),
        compiler_params=pltpu.CompilerParams(vmem_limit_bytes=32 * 1024 * 1024),
        cost_estimate=pl.CostEstimate(flops=300_000, bytes_accessed=2_500_000, transcendentals=0),
    )(fields, na, top)


def solution(mesh):
    in_specs = (P(None, "gz", "gy", None), P(None, "gz", "gy", None))
    out_specs = (P(None, "gz", "gy", None), P(None, "gz", "gy", None), P())
    return jax.shard_map(local, mesh=mesh, in_specs=in_specs, out_specs=out_specs, check_vma=False)
```

```python
import jax
import jax.numpy as jnp
from jax import lax
from jax.experimental import pallas as pl
from jax.experimental.pallas import tpu as pltpu
from jax.sharding import PartitionSpec as P

MESH = pl.DeviceIdType.MESH
F32 = jnp.float32
MIXED = (2, 3, 6, 7)
COLUMN = 8
PLANE = 128


def chief(index):
    at = (index + 1) % PLANE
    return at // 8, at % 8


def hops(index):
    gy, gz = chief(index)
    x, y = gy // 2, gy % 2 * 4 + gz // 2
    return min(x, 8 - x) + min(y, 8 - y)


NEAR_FIRST = sorted(range(1, PLANE), key=hops)


def x_shift(t, s):
    return pltpu.roll(t, (256 - s) % 256, 1)


def y_shift(t, h, s):
    row = lax.broadcasted_iota(jnp.int32, t.shape, 0)
    if s > 0:
        return pltpu.roll(jnp.where(row < s, h, t), 8 - s, 0)
    return pltpu.roll(jnp.where(row >= 8 + s, h, t), -s, 0)


def first_of(f):
    return (
        (45.0 / 60.0) * (f(1) - f(-1))
        - (9.0 / 60.0) * (f(2) - f(-2))
        + (1.0 / 60.0) * (f(3) - f(-3))
    )


def second_of(f):
    return (
        (-490.0 / 180.0) * f(0)
        + (270.0 / 180.0) * (f(1) + f(-1))
        - (27.0 / 180.0) * (f(2) + f(-2))
        + (2.0 / 180.0) * (f(3) + f(-3))
    )


def memo(f):
    held = {}

    def get(s):
        if s not in held:
            held[s] = f(s)
        return held[s]

    return get


def along_x(t):
    return memo(lambda s: t if s == 0 else x_shift(t, s))


def substep(
    f_hbm,
    a_hbm,
    na_ref,
    top_ref,
    F,
    A,
    H,
    GY,
    B,
    tile,
    own,
    ups,
    chiefs,
    down,
    load_sem,
    y_send,
    y_recv,
    z_send,
    z_recv,
    c_send,
    c_recv,
    t_send,
    t_recv,
):
    gy = lax.axis_index("gy")
    gz = lax.axis_index("gz")
    up_y, down_y = lax.rem(gy + 1, 16), lax.rem(gy + 15, 16)
    up_z, down_z = lax.rem(gz + 1, 64), lax.rem(gz + 63, 64)
    level = gz // 8
    among = lax.rem(gy * 8 + gz + PLANE - 1, PLANE)
    is_chief = level == 0
    is_root = jnp.logical_and(gy == 0, gz == 1)

    load_f = pltpu.make_async_copy(f_hbm, F.at[:, pl.ds(3, 8)], load_sem.at[0])
    load_a = pltpu.make_async_copy(a_hbm, A, load_sem.at[1])
    load_f.start()
    load_a.start()

    barrier = pltpu.get_barrier_semaphore()
    for to in ((up_y, gz), (down_y, gz), (gy, up_z), (gy, down_z)):
        pl.semaphore_signal(barrier, inc=1, device_id=to, device_id_type=MESH)

    @pl.when(is_root)
    def _():
        for i in [0, *NEAR_FIRST]:
            pl.semaphore_signal(barrier, inc=1, device_id=chief(i), device_id_type=MESH)

    @pl.when(is_chief)
    def _():
        for i in range(1, COLUMN):
            pl.semaphore_signal(barrier, inc=1, device_id=(gy, gz + 8 * i), device_id_type=MESH)

    pl.semaphore_wait(barrier, 5)

    def remote(src, dst, send, recv, to):
        return pltpu.make_async_remote_copy(
            src_ref=src, dst_ref=dst, send_sem=send, recv_sem=recv, device_id=to, device_id_type=MESH
        )

    low, high = pl.ds(0, 3), pl.ds(5, 3)

    def y_halo(part, start, count):
        ks = pl.ds(start, count)
        return [
            remote(f_hbm.at[ks, :, low], H.at[ks, pl.ds(3, 8), low], y_send.at[0, part], y_recv.at[0, part], (down_y, gz)),
            remote(f_hbm.at[ks, :, high], H.at[ks, pl.ds(3, 8), high], y_send.at[1, part], y_recv.at[1, part], (up_y, gz)),
        ]

    def z_halo(part, start, count):
        ks = pl.ds(start, count)
        return [
            remote(f_hbm.at[ks, low], F.at[ks, pl.ds(11, 3)], z_send.at[0, part], z_recv.at[0, part], (gy, down_z)),
            remote(f_hbm.at[ks, high], F.at[ks, pl.ds(0, 3)], z_send.at[1, part], z_recv.at[1, part], (gy, up_z)),
        ]

    def corner(part, start):
        ks, near, far = pl.ds(start, 2), pl.ds(0, 3), pl.ds(11, 3)
        return [
            remote(F.at[ks, near, low], H.at[ks, near, low], c_send.at[0, part], c_recv.at[0, part], (down_y, gz)),
            remote(F.at[ks, near, high], H.at[ks, near, high], c_send.at[1, part], c_recv.at[1, part], (up_y, gz)),
            remote(F.at[ks, far, low], H.at[ks, far, low], c_send.at[2, part], c_recv.at[2, part], (down_y, gz)),
            remote(F.at[ks, far, high], H.at[ks, far, high], c_send.at[3, part], c_recv.at[3, part], (up_y, gz)),
        ]

    first = y_halo(0, 5, 1) + y_halo(1, 7, 1) + z_halo(0, 5, 2)
    then_z = z_halo(1, 7, 1) + z_halo(2, 0, 5)
    then_y = y_halo(2, 6, 1) + y_halo(3, 0, 5)
    corners = corner(0, 2) + corner(1, 6)
    for copy in first + then_z:
        copy.start()

    def along_y(k, i):
        t, h = F[k, i + 3], H[k, i + 3]
        return memo(lambda s: t if s == 0 else y_shift(t, h, s))

    def along_z(k, i):
        return lambda s: F[k, i + 3 + s]

    load_f.wait()
    for copy in first:
        copy.wait_recv()

    tile[...] = jnp.zeros_like(tile)

    def rates(i, c):
        t = [F[k, i + 3] for k in range(8)]
        bx = first_of(along_y(7, i)) - first_of(along_z(6, i))
        by = first_of(along_z(5, i)) - first_of(along_x(t[7]))
        bz = first_of(along_x(t[6])) - first_of(along_y(5, i))
        B[0, i] = bx
        B[1, i] = by
        B[2, i] = bz
        cs2 = jnp.exp((5.0 / 3.0) * t[4] + (2.0 / 3.0) * t[0])
        inverse = jnp.exp(-t[0])
        rate = (
            jnp.abs(t[1])
            + jnp.abs(t[2])
            + jnp.abs(t[3])
            + jnp.sqrt(cs2 + (bx * bx + by * by + bz * bz) * inverse)
        )
        tile[...] = jnp.maximum(tile[...], jnp.maximum(rate[:, :128], rate[:, 128:]))
        return c

    lax.fori_loop(0, 8, rates, 0)

    own[...] = jnp.max(tile[...], axis=0, keepdims=True)
    chief_id = (gy, lax.rem(gz, 8))
    to_chief = remote(own, ups.at[level], t_send.at[0], t_recv.at[0], chief_id)
    all_ups = remote(ups.at[pl.ds(1, COLUMN - 1)], ups.at[pl.ds(1, COLUMN - 1)], t_send.at[2], t_recv.at[0], chief_id)
    to_root = remote(own, chiefs.at[among], t_send.at[1], t_recv.at[1], chief(0))
    all_chiefs = remote(chiefs.at[pl.ds(1, PLANE - 1)], chiefs.at[pl.ds(1, PLANE - 1)], t_send.at[3], t_recv.at[1], chief(0))
    to_down = remote(down, down, t_send.at[2], t_recv.at[2], chief(0))

    @pl.when(jnp.logical_not(is_chief))
    def _():
        to_chief.start()

    for copy in then_y:
        copy.start()

    def forward():
        for copy in then_z:
            copy.wait_recv()
        for copy in corners:
            copy.start()

    pl.when(gz != 0)(forward)

    @pl.when(is_chief)
    def _():
        all_ups.wait_recv()
        own[...] = jnp.maximum(own[...], jnp.max(ups[1:], axis=0))

        @pl.when(jnp.logical_not(is_root))
        def _():
            to_root.start()

    pl.when(gz == 0)(forward)

    load_a.wait()
    for copy in then_y + corners:
        copy.wait_recv()

    def slopes(i, c):
        for j, k in enumerate(MIXED):
            GY[j, i] = first_of(along_y(k, i - 3))
        return c

    lax.fori_loop(0, 14, slopes, 0)

    def partial(i, c):
        t = [F[k, i + 3] for k in range(8)]
        ax = [along_x(t[k]) for k in range(8)]
        ay = [along_y(k, i) for k in range(8)]
        az = [along_z(k, i) for k in range(8)]
        dx = {k: first_of(ax[k]) for k in range(5)}
        dy = {k: GY[MIXED.index(k), i + 3] if k in MIXED else first_of(ay[k]) for k in range(7)}
        dz = {k: first_of(az[k]) for k in (0, 1, 2, 3, 4, 5, 7)}
        u = t[1:4]
        bx, by, bz = B[0, i], B[1, i], B[2, i]
        yz = [first_of(lambda s, j=j: GY[j, i + 3 + s]) for j in range(4)]
        inverse = jnp.exp(-t[0])

        def put(k, value):
            na_ref[k, i] = (-5.0 / 9.0) * A[k, i] + value

        def advect(k):
            return u[0] * dx[k] + u[1] * dy[k] + u[2] * dz[k]

        divu = dx[1] + dy[2] + dz[3]
        third = divu * (1.0 / 3.0)
        sxx, syy, szz = dx[1] - third, dy[2] - third, dz[3] - third
        sxy = 0.5 * (dy[1] + dx[2])
        sxz = 0.5 * (dz[1] + dx[3])
        syz = 0.5 * (dz[2] + dy[3])
        cs2 = jnp.exp((5.0 / 3.0) * t[4] + (2.0 / 3.0) * t[0])
        put(0, -advect(0) - divu)
        strain = ((sxx, sxy, sxz), (sxy, syy, syz), (sxz, syz, szz))
        axx = second_of(ax[5]), second_of(ax[6]), second_of(ax[7])
        ayy = second_of(ay[5]), second_of(ay[6]), second_of(ay[7])
        azz = second_of(az[5]), second_of(az[6]), second_of(az[7])
        jx = first_of(along_x(dy[6])) + first_of(along_x(dz[7])) - ayy[0] - azz[0]
        jy = first_of(along_x(dy[5])) + yz[3] - axx[1] - azz[1]
        jz = first_of(along_x(dz[5])) + yz[2] - axx[2] - ayy[2]
        lorentz = (jy * bz - jz * by, jz * bx - jx * bz, jx * by - jy * bx)
        xx = second_of(ax[1]), second_of(ax[2]), second_of(ax[3])
        yy = second_of(ay[1]), second_of(ay[2]), second_of(ay[3])
        zz = second_of(az[1]), second_of(az[2]), second_of(az[3])
        mixed = (
            xx[0] + first_of(along_x(dy[2])) + first_of(along_x(dz[3])),
            yy[1] + first_of(along_x(dy[1])) + yz[1],
            zz[2] + first_of(along_x(dz[1])) + yz[0],
        )
        grad = (dx, dy, dz)
        for n in range(3):
            viscous = (
                xx[n]
                + yy[n]
                + zz[n]
                + mixed[n] * (1.0 / 3.0)
                + 2.0 * (strain[n][0] * dx[0] + strain[n][1] * dy[0] + strain[n][2] * dz[0])
            )
            put(
                1 + n,
                -advect(1 + n) - cs2 * (grad[n][4] + grad[n][0]) + lorentz[n] * inverse + 0.1 * viscous,
            )
        norm = sxx * sxx + syy * syy + szz * szz + 2.0 * (sxy * sxy + sxz * sxz + syz * syz)
        heat = 0.2 * norm + 0.1 * (jx * jx + jy * jy + jz * jz) * inverse
        put(4, -advect(4) + heat / (1.5 * cs2))

        cross = (u[1] * bz - u[2] * by, u[2] * bx - u[0] * bz, u[0] * by - u[1] * bx)
        for n in range(3):
            put(5 + n, cross[n] + 0.1 * (axx[n] + ayy[n] + azz[n]))
        return c

    lax.fori_loop(0, 8, partial, 0)

    @pl.when(is_root)
    def _():
        all_chiefs.wait_recv()
        most = jnp.max(jnp.maximum(own[...], jnp.max(chiefs[1:], axis=0)))
        down[...] = jnp.full(down.shape, most, F32)
        for i in NEAR_FIRST:
            remote(down, down, t_send.at[3], t_recv.at[2], chief(i)).start()

    @pl.when(jnp.logical_not(is_root))
    def _():
        to_down.wait_recv()

    @pl.when(is_chief)
    def _():
        for i in range(1, COLUMN):
            remote(down, down, t_send.at[2], t_recv.at[2], (gy, gz + 8 * i)).start()

    top_ref[...] = down[...]

    for copy in first + then_y + then_z + corners:
        copy.wait_send()

    @pl.when(jnp.logical_not(is_chief))
    def _():
        to_chief.wait_send()

    @pl.when(is_chief)
    def _():
        all_ups.wait_send()

        @pl.when(jnp.logical_not(is_root))
        def _():
            to_root.wait_send()

    @pl.when(is_root)
    def _():
        all_chiefs.wait_send()


def update(f_ref, na_ref, top_ref, nf_ref, out_ref, dt_ref):
    dt = 0.4 / top_ref[...]
    dt_ref[0] = dt[0, 0]
    scale = (15.0 / 16.0) * dt[:, 0:1]
    na = na_ref[...]
    out_ref[...] = na
    nf_ref[...] = f_ref[...] + scale[None, None] * na


def local(fields, accum):
    block = jax.ShapeDtypeStruct(fields.shape, F32)
    vmem = pl.BlockSpec(memory_space=pltpu.VMEM)
    anywhere = pl.BlockSpec(memory_space=pl.ANY)
    na, top = pl.pallas_call(
        substep,
        out_shape=(pltpu.VMEM(fields.shape, F32), pltpu.VMEM((1, 128), F32)),
        in_specs=[anywhere, anywhere],
        out_specs=(vmem, vmem),
        scratch_shapes=[
            pltpu.VMEM((8, 14, 8, 256), F32),
            pltpu.VMEM((8, 8, 8, 256), F32),
            pltpu.VMEM((8, 14, 8, 256), F32),
            pltpu.VMEM((4, 14, 8, 256), F32),
            pltpu.VMEM((3, 8, 8, 256), F32),
            pltpu.VMEM((8, 128), F32),
            pltpu.VMEM((1, 128), F32),
            pltpu.VMEM((COLUMN, 1, 128), F32),
            pltpu.VMEM((PLANE, 1, 128), F32),
            pltpu.VMEM((1, 128), F32),
            pltpu.SemaphoreType.DMA((2,)),
            pltpu.SemaphoreType.DMA((2, 4)),
            pltpu.SemaphoreType.DMA((2, 4)),
            pltpu.SemaphoreType.DMA((2, 3)),
            pltpu.SemaphoreType.DMA((2, 3)),
            pltpu.SemaphoreType.DMA((4, 2)),
            pltpu.SemaphoreType.DMA((4, 2)),
            pltpu.SemaphoreType.DMA((4,)),
            pltpu.SemaphoreType.DMA((3,)),
        ],
        compiler_params=pltpu.CompilerParams(
            collective_id=0, has_side_effects=True, vmem_limit_bytes=60 * 1024 * 1024
        ),
        cost_estimate=pl.CostEstimate(flops=13_000_000, bytes_accessed=2_000_000, transcendentals=100_000),
    )(fields, accum)
    return pl.pallas_call(
        update,
        out_shape=(block, block, jax.ShapeDtypeStruct((1,), F32)),
        in_specs=[vmem, vmem, vmem],
        out_specs=(vmem, vmem, pl.BlockSpec(memory_space=pltpu.SMEM)),
        compiler_params=pltpu.CompilerParams(vmem_limit_bytes=32 * 1024 * 1024),
        cost_estimate=pl.CostEstimate(flops=300_000, bytes_accessed=2_500_000, transcendentals=0),
    )(fields, na, top)


def solution(mesh):
    in_specs = (P(None, "gz", "gy", None), P(None, "gz", "gy", None))
    out_specs = (P(None, "gz", "gy", None), P(None, "gz", "gy", None), P())
    return jax.shard_map(local, mesh=mesh, in_specs=in_specs, out_specs=out_specs, check_vma=False)
```

```python
import jax
import jax.numpy as jnp
from jax import lax
from jax.experimental import pallas as pl
from jax.experimental.pallas import tpu as pltpu
from jax.sharding import PartitionSpec as P

MESH = pl.DeviceIdType.MESH
F32 = jnp.float32
MIXED = (2, 3, 6, 7)
FIRST, SECOND = (0, 1), (2, 0)
COLUMN = 8
PLANE = 128


def chief(index):
    at = (index + 1) % PLANE
    return at // 8, at % 8


def hops(index):
    gy, gz = chief(index)
    x, y = gy // 2, gy % 2 * 4 + gz // 2
    return min(x, 8 - x) + min(y, 8 - y)


NEAR_FIRST = sorted(range(1, PLANE), key=hops)


def x_shift(t, s):
    return pltpu.roll(t, (256 - s) % 256, 1)


def y_shift(t, h, s):
    row = lax.broadcasted_iota(jnp.int32, t.shape, 0)
    if s > 0:
        return pltpu.roll(jnp.where(row < s, h, t), 8 - s, 0)
    return pltpu.roll(jnp.where(row >= 8 + s, h, t), -s, 0)


def first_of(f):
    return (
        (45.0 / 60.0) * (f(1) - f(-1))
        - (9.0 / 60.0) * (f(2) - f(-2))
        + (1.0 / 60.0) * (f(3) - f(-3))
    )


def second_of(f):
    return (
        (-490.0 / 180.0) * f(0)
        + (270.0 / 180.0) * (f(1) + f(-1))
        - (27.0 / 180.0) * (f(2) + f(-2))
        + (2.0 / 180.0) * (f(3) + f(-3))
    )


def memo(f):
    held = {}

    def get(s):
        if s not in held:
            held[s] = f(s)
        return held[s]

    return get


def along_x(t):
    return memo(lambda s: t if s == 0 else x_shift(t, s))


def substep(
    f_hbm,
    a_hbm,
    na_ref,
    top_ref,
    F,
    A,
    H,
    GY,
    B,
    tile,
    own,
    ups,
    chiefs,
    down,
    load_sem,
    y_send,
    y_recv,
    z_send,
    z_recv,
    c_send,
    c_recv,
    t_send,
    t_recv,
):
    gy = lax.axis_index("gy")
    gz = lax.axis_index("gz")
    up_y, down_y = lax.rem(gy + 1, 16), lax.rem(gy + 15, 16)
    up_z, down_z = lax.rem(gz + 1, 64), lax.rem(gz + 63, 64)
    level = gz // 8
    among = lax.rem(gy * 8 + gz + PLANE - 1, PLANE)
    is_chief = level == 0
    is_first = jnp.logical_and(gy == 0, gz == 1)
    is_second = jnp.logical_and(gy == 2, gz == 0)
    is_root = jnp.logical_or(is_first, is_second)

    load_f = pltpu.make_async_copy(f_hbm, F.at[:, pl.ds(3, 8)], load_sem.at[0])
    load_a = pltpu.make_async_copy(a_hbm, A, load_sem.at[1])
    load_f.start()
    load_a.start()

    barrier = pltpu.get_barrier_semaphore()
    for to in ((up_y, gz), (down_y, gz), (gy, up_z), (gy, down_z)):
        pl.semaphore_signal(barrier, inc=1, device_id=to, device_id_type=MESH)

    @pl.when(is_root)
    def _():
        for i in [0, *NEAR_FIRST]:
            pl.semaphore_signal(barrier, inc=1, device_id=chief(i), device_id_type=MESH)

    @pl.when(is_chief)
    def _():
        for i in range(1, COLUMN):
            pl.semaphore_signal(barrier, inc=1, device_id=(gy, gz + 8 * i), device_id_type=MESH)

    @pl.when(is_chief)
    def _():
        pl.semaphore_wait(barrier, 6)

    @pl.when(jnp.logical_not(is_chief))
    def _():
        pl.semaphore_wait(barrier, 5)

    def remote(src, dst, send, recv, to):
        return pltpu.make_async_remote_copy(
            src_ref=src, dst_ref=dst, send_sem=send, recv_sem=recv, device_id=to, device_id_type=MESH
        )

    low, high = pl.ds(0, 3), pl.ds(5, 3)

    def y_halo(part, start, count):
        ks = pl.ds(start, count)
        return [
            remote(f_hbm.at[ks, :, low], H.at[ks, pl.ds(3, 8), low], y_send.at[0, part], y_recv.at[0, part], (down_y, gz)),
            remote(f_hbm.at[ks, :, high], H.at[ks, pl.ds(3, 8), high], y_send.at[1, part], y_recv.at[1, part], (up_y, gz)),
        ]

    def z_halo(part, start, count):
        ks = pl.ds(start, count)
        return [
            remote(f_hbm.at[ks, low], F.at[ks, pl.ds(11, 3)], z_send.at[0, part], z_recv.at[0, part], (gy, down_z)),
            remote(f_hbm.at[ks, high], F.at[ks, pl.ds(0, 3)], z_send.at[1, part], z_recv.at[1, part], (gy, up_z)),
        ]

    def corner(part, start):
        ks, near, far = pl.ds(start, 2), pl.ds(0, 3), pl.ds(11, 3)
        return [
            remote(F.at[ks, near, low], H.at[ks, near, low], c_send.at[0, part], c_recv.at[0, part], (down_y, gz)),
            remote(F.at[ks, near, high], H.at[ks, near, high], c_send.at[1, part], c_recv.at[1, part], (up_y, gz)),
            remote(F.at[ks, far, low], H.at[ks, far, low], c_send.at[2, part], c_recv.at[2, part], (down_y, gz)),
            remote(F.at[ks, far, high], H.at[ks, far, high], c_send.at[3, part], c_recv.at[3, part], (up_y, gz)),
        ]

    first = y_halo(0, 5, 1) + y_halo(1, 7, 1) + z_halo(0, 5, 2)
    then_z = z_halo(1, 7, 1) + z_halo(2, 0, 5)
    then_y = y_halo(2, 6, 1) + y_halo(3, 0, 5)
    corners = corner(0, 2) + corner(1, 6)
    for copy in first + then_z:
        copy.start()

    def along_y(k, i):
        t, h = F[k, i + 3], H[k, i + 3]
        return memo(lambda s: t if s == 0 else y_shift(t, h, s))

    def along_z(k, i):
        return lambda s: F[k, i + 3 + s]

    load_f.wait()
    for copy in first:
        copy.wait_recv()

    tile[...] = jnp.zeros_like(tile)

    def rates(i, c):
        t = [F[k, i + 3] for k in range(8)]
        bx = first_of(along_y(7, i)) - first_of(along_z(6, i))
        by = first_of(along_z(5, i)) - first_of(along_x(t[7]))
        bz = first_of(along_x(t[6])) - first_of(along_y(5, i))
        B[0, i] = bx
        B[1, i] = by
        B[2, i] = bz
        cs2 = jnp.exp((5.0 / 3.0) * t[4] + (2.0 / 3.0) * t[0])
        inverse = jnp.exp(-t[0])
        rate = (
            jnp.abs(t[1])
            + jnp.abs(t[2])
            + jnp.abs(t[3])
            + jnp.sqrt(cs2 + (bx * bx + by * by + bz * bz) * inverse)
        )
        tile[...] = jnp.maximum(tile[...], jnp.maximum(rate[:, :128], rate[:, 128:]))
        return c

    lax.fori_loop(0, 8, rates, 0)

    own[...] = jnp.max(tile[...], axis=0, keepdims=True)
    chief_id = (gy, lax.rem(gz, 8))
    to_chief = remote(own, ups.at[level], t_send.at[0], t_recv.at[0], chief_id)
    all_ups = remote(ups.at[pl.ds(1, COLUMN - 1)], ups.at[pl.ds(1, COLUMN - 1)], t_send.at[2], t_recv.at[0], chief_id)
    to_first = remote(own, chiefs.at[among], t_send.at[1], t_recv.at[1], FIRST)
    to_second = remote(own, chiefs.at[among], t_send.at[4], t_recv.at[1], SECOND)
    all_chiefs = remote(chiefs.at[pl.ds(1, PLANE - 1)], chiefs.at[pl.ds(1, PLANE - 1)], t_send.at[3], t_recv.at[1], chief(0))
    half_sends = remote(chiefs.at[pl.ds(1, PLANE // 2 - 1)], chiefs.at[pl.ds(1, PLANE // 2 - 1)], t_send.at[3], t_recv.at[1], chief(0))
    to_down = remote(down, down, t_send.at[2], t_recv.at[2], chief(0))

    @pl.when(jnp.logical_not(is_chief))
    def _():
        to_chief.start()

    for copy in then_y:
        copy.start()

    def forward():
        for copy in then_z:
            copy.wait_recv()
        for copy in corners:
            copy.start()

    pl.when(gz != 0)(forward)

    @pl.when(is_chief)
    def _():
        all_ups.wait_recv()
        own[...] = jnp.maximum(own[...], jnp.max(ups[1:], axis=0))

        @pl.when(jnp.logical_not(is_first))
        def _():
            to_first.start()

        @pl.when(jnp.logical_not(is_second))
        def _():
            to_second.start()

    pl.when(gz == 0)(forward)

    load_a.wait()
    for copy in then_y + corners:
        copy.wait_recv()

    def slopes(i, c):
        for j, k in enumerate(MIXED):
            GY[j, i] = first_of(along_y(k, i - 3))
        return c

    lax.fori_loop(0, 14, slopes, 0)

    def partial(i, c):
        t = [F[k, i + 3] for k in range(8)]
        ax = [along_x(t[k]) for k in range(8)]
        ay = [along_y(k, i) for k in range(8)]
        az = [along_z(k, i) for k in range(8)]
        dx = {k: first_of(ax[k]) for k in range(5)}
        dy = {k: GY[MIXED.index(k), i + 3] if k in MIXED else first_of(ay[k]) for k in range(7)}
        dz = {k: first_of(az[k]) for k in (0, 1, 2, 3, 4, 5, 7)}
        u = t[1:4]
        bx, by, bz = B[0, i], B[1, i], B[2, i]
        yz = [first_of(lambda s, j=j: GY[j, i + 3 + s]) for j in range(4)]
        inverse = jnp.exp(-t[0])

        def put(k, value):
            na_ref[k, i] = (-5.0 / 9.0) * A[k, i] + value

        def advect(k):
            return u[0] * dx[k] + u[1] * dy[k] + u[2] * dz[k]

        divu = dx[1] + dy[2] + dz[3]
        third = divu * (1.0 / 3.0)
        sxx, syy, szz = dx[1] - third, dy[2] - third, dz[3] - third
        sxy = 0.5 * (dy[1] + dx[2])
        sxz = 0.5 * (dz[1] + dx[3])
        syz = 0.5 * (dz[2] + dy[3])
        cs2 = jnp.exp((5.0 / 3.0) * t[4] + (2.0 / 3.0) * t[0])
        put(0, -advect(0) - divu)
        strain = ((sxx, sxy, sxz), (sxy, syy, syz), (sxz, syz, szz))
        axx = second_of(ax[5]), second_of(ax[6]), second_of(ax[7])
        ayy = second_of(ay[5]), second_of(ay[6]), second_of(ay[7])
        azz = second_of(az[5]), second_of(az[6]), second_of(az[7])
        jx = first_of(along_x(dy[6])) + first_of(along_x(dz[7])) - ayy[0] - azz[0]
        jy = first_of(along_x(dy[5])) + yz[3] - axx[1] - azz[1]
        jz = first_of(along_x(dz[5])) + yz[2] - axx[2] - ayy[2]
        lorentz = (jy * bz - jz * by, jz * bx - jx * bz, jx * by - jy * bx)
        xx = second_of(ax[1]), second_of(ax[2]), second_of(ax[3])
        yy = second_of(ay[1]), second_of(ay[2]), second_of(ay[3])
        zz = second_of(az[1]), second_of(az[2]), second_of(az[3])
        mixed = (
            xx[0] + first_of(along_x(dy[2])) + first_of(along_x(dz[3])),
            yy[1] + first_of(along_x(dy[1])) + yz[1],
            zz[2] + first_of(along_x(dz[1])) + yz[0],
        )
        grad = (dx, dy, dz)
        for n in range(3):
            viscous = (
                xx[n]
                + yy[n]
                + zz[n]
                + mixed[n] * (1.0 / 3.0)
                + 2.0 * (strain[n][0] * dx[0] + strain[n][1] * dy[0] + strain[n][2] * dz[0])
            )
            put(
                1 + n,
                -advect(1 + n) - cs2 * (grad[n][4] + grad[n][0]) + lorentz[n] * inverse + 0.1 * viscous,
            )
        norm = sxx * sxx + syy * syy + szz * szz + 2.0 * (sxy * sxy + sxz * sxz + syz * syz)
        heat = 0.2 * norm + 0.1 * (jx * jx + jy * jy + jz * jz) * inverse
        put(4, -advect(4) + heat / (1.5 * cs2))

        cross = (u[1] * bz - u[2] * by, u[2] * bx - u[0] * bz, u[0] * by - u[1] * bx)
        for n in range(3):
            put(5 + n, cross[n] + 0.1 * (axx[n] + ayy[n] + azz[n]))
        return c

    lax.fori_loop(0, 8, partial, 0)

    @pl.when(is_root)
    def _():
        all_chiefs.wait_recv()
        chiefs[among] = own[...]
        most = jnp.max(jnp.max(chiefs[...], axis=0))
        down[...] = jnp.full(down.shape, most, F32)

    for when, core in ((is_first, 1), (is_second, 0)):

        @pl.when(when)
        def _():
            for i in [0, *NEAR_FIRST]:
                to = chief(i)
                if to[1] % 2 == core and to not in (FIRST, SECOND):
                    remote(down, down, t_send.at[3], t_recv.at[2], to).start()

    @pl.when(jnp.logical_not(is_root))
    def _():
        to_down.wait_recv()

    @pl.when(is_chief)
    def _():
        for i in range(1, COLUMN):
            remote(down, down, t_send.at[2], t_recv.at[2], (gy, gz + 8 * i)).start()

    top_ref[...] = down[...]

    for copy in first + then_y + then_z + corners:
        copy.wait_send()

    @pl.when(jnp.logical_not(is_chief))
    def _():
        to_chief.wait_send()

    @pl.when(is_chief)
    def _():
        all_ups.wait_send()

        @pl.when(jnp.logical_not(is_first))
        def _():
            to_first.wait_send()

        @pl.when(jnp.logical_not(is_second))
        def _():
            to_second.wait_send()

    @pl.when(is_root)
    def _():
        half_sends.wait_send()


def update(f_ref, na_ref, top_ref, nf_ref, out_ref, dt_ref):
    dt = 0.4 / top_ref[...]
    dt_ref[0] = dt[0, 0]
    scale = (15.0 / 16.0) * dt[:, 0:1]
    na = na_ref[...]
    out_ref[...] = na
    nf_ref[...] = f_ref[...] + scale[None, None] * na


def local(fields, accum):
    block = jax.ShapeDtypeStruct(fields.shape, F32)
    vmem = pl.BlockSpec(memory_space=pltpu.VMEM)
    anywhere = pl.BlockSpec(memory_space=pl.ANY)
    na, top = pl.pallas_call(
        substep,
        out_shape=(pltpu.VMEM(fields.shape, F32), pltpu.VMEM((1, 128), F32)),
        in_specs=[anywhere, anywhere],
        out_specs=(vmem, vmem),
        scratch_shapes=[
            pltpu.VMEM((8, 14, 8, 256), F32),
            pltpu.VMEM((8, 8, 8, 256), F32),
            pltpu.VMEM((8, 14, 8, 256), F32),
            pltpu.VMEM((4, 14, 8, 256), F32),
            pltpu.VMEM((3, 8, 8, 256), F32),
            pltpu.VMEM((8, 128), F32),
            pltpu.VMEM((1, 128), F32),
            pltpu.VMEM((COLUMN, 1, 128), F32),
            pltpu.VMEM((PLANE, 1, 128), F32),
            pltpu.VMEM((1, 128), F32),
            pltpu.SemaphoreType.DMA((2,)),
            pltpu.SemaphoreType.DMA((2, 4)),
            pltpu.SemaphoreType.DMA((2, 4)),
            pltpu.SemaphoreType.DMA((2, 3)),
            pltpu.SemaphoreType.DMA((2, 3)),
            pltpu.SemaphoreType.DMA((4, 2)),
            pltpu.SemaphoreType.DMA((4, 2)),
            pltpu.SemaphoreType.DMA((5,)),
            pltpu.SemaphoreType.DMA((3,)),
        ],
        compiler_params=pltpu.CompilerParams(
            collective_id=0, has_side_effects=True, vmem_limit_bytes=60 * 1024 * 1024
        ),
        cost_estimate=pl.CostEstimate(flops=13_000_000, bytes_accessed=2_000_000, transcendentals=100_000),
    )(fields, accum)
    return pl.pallas_call(
        update,
        out_shape=(block, block, jax.ShapeDtypeStruct((1,), F32)),
        in_specs=[vmem, vmem, vmem],
        out_specs=(vmem, vmem, pl.BlockSpec(memory_space=pltpu.SMEM)),
        compiler_params=pltpu.CompilerParams(vmem_limit_bytes=32 * 1024 * 1024),
        cost_estimate=pl.CostEstimate(flops=300_000, bytes_accessed=2_500_000, transcendentals=0),
    )(fields, na, top)


def solution(mesh):
    in_specs = (P(None, "gz", "gy", None), P(None, "gz", "gy", None))
    out_specs = (P(None, "gz", "gy", None), P(None, "gz", "gy", None), P())
    return jax.shard_map(local, mesh=mesh, in_specs=in_specs, out_specs=out_specs, check_vma=False)
```
